1024 devices in a mesh: group: 32 (over x_lo, y, core), tp: 32 (over z, x_hi).
Axes of the slice: x: 8 (x_hi: 4, x_lo: 2; x = x_hi * 2 + x_lo), y: 8, z: 8, core: 2. Of those that a mesh axis runs over, the one named last changes fastest.
Arguments:
- acts: bfloat16 [1024, 8, 4096], P('group'), may hold values from -6 to 6
- gate_weight: bfloat16 [4096, 15360], P('group', 'tp'), may hold values from -0.09375 to 0.09375
- up_weight: bfloat16 [4096, 15360], P('group', 'tp'), may hold values from -0.09375 to 0.09375
- section_weight: bfloat16 [32, 15360, 512], P('group', 'tp'), may hold values from -0.046875 to 0.046875
- readout: float32 [32, 512], P('group'), may hold values from -0.25 to 0.25
- lengths: int32 [1024], P('group'), may hold values from 1 to 8
- routing: int32 [32, 32], P('group'), may hold values from 0 to 31, each once within a row
Outputs:
- scores: float32 [1024, 8], P('group')
The draws below stay inside these ranges and needn't reach their ends.
Inputs may be any that keep to these rules, and one draw needn't show every extreme that they name: `routing`: each row is an ordering of its group's 32 local rollouts.
All inputs are finite; a program needn't handle non-finite values.
Results may differ from the reference program's by a relative error of at most 0.0031.
Values may be sent and summed in bfloat16 or wider, within the bound.
No kernel may reach another device: no remote copies, remote signals or barrier semaphores. Data moves between devices by JAX's collectives and lax.ppermute only.
A program may use at most 32 MiB of HBM per device.

```python
import jax
import jax.numpy as jnp
from jax import lax

D = 4096
E = 512
STEPS = 8
BLK = 1
ROLL = 32
ROLLOUTS = 1024
F = 15360
N_GROUP = 32


def plant(array, rng, least, high):
    extent = array.shape
    spot = [jax.random.randint(jax.random.fold_in(rng, axis), (), 0, extent[axis]) for axis in range(len(extent))]
    array = array.at[tuple(spot)].set(least)
    longest = extent.index(max(extent))
    spot[longest] = (spot[longest] + 1) % extent[longest]
    return array.at[tuple(spot)].set(high)


def block_levels(key, shape, shards, smallest, top_value):
    level, own = 1.0, jax.random.fold_in(key, 6)
    for axis_at, shards_of in shards:
        heights = jnp.exp(jax.random.uniform(jax.random.fold_in(own, axis_at), (shards_of,), jnp.float32, smallest / len(shards), top_value / len(shards)))
        level = level * jnp.repeat(heights, shape[axis_at] // shards_of).reshape([-1 if axis == axis_at else 1 for axis in range(len(shape))])
    return level


def noise(own_key, shape, deviation, most, split=(), held_as=jnp.bfloat16):
    drawn = jax.random.normal(own_key, shape, jnp.float32) * deviation
    if len(split) > 0:
        drawn = block_levels(own_key, shape, split, -0.22, 0.18) * drawn
    return jnp.clip(drawn, min=-most, max=most).astype(held_as)


def setup_inputs(seed: int = 0) -> dict:
    keys = jax.random.split(jax.random.key(seed), 8)
    acts = noise(keys[0], (ROLLOUTS, STEPS, D), 1.0, 6.0, ((0, 32),))
    gate_weight = noise(keys[1], (D, F), D ** -0.5, 0.09375, ((0, 32), (1, 32)))
    up_weight = noise(keys[2], (D, F), D ** -0.5, 0.09375, ((0, 32), (1, 32)))
    section_weight = noise(keys[3], (N_GROUP, F, E), F ** -0.5, 0.046875, ((0, 32), (1, 32)))
    readout = noise(keys[4], (N_GROUP, E), E ** -0.5, 0.25, ((0, 32),), jnp.float32)
    lengths = plant(jax.random.randint(keys[5], (ROLLOUTS,), 1, STEPS + 1), jax.random.fold_in(keys[5], 1), 1, STEPS).astype(jnp.int32)
    routing = jax.vmap(lambda own: jax.random.permutation(own, ROLL))(jax.random.split(keys[6], N_GROUP)).reshape((N_GROUP, ROLL)).astype(jnp.int32)
    return {"acts": acts, "gate_weight": gate_weight, "up_weight": up_weight, "section_weight": section_weight, "readout": readout, "lengths": lengths, "routing": routing}


def reference(acts, gate_weight, up_weight, section_weight, readout, lengths, routing):
    rollouts, steps, width = acts.shape
    units = gate_weight.shape[1]
    blocks = acts.reshape(N_GROUP, ROLL * steps, width)

    def actor(block):
        gate = jnp.dot(block, gate_weight, preferred_element_type=jnp.float32)
        up = jnp.dot(block, up_weight, preferred_element_type=jnp.float32)
        return (jax.nn.silu(gate) * up).astype(jnp.bfloat16)

    hidden = lax.map(actor, blocks).reshape(N_GROUP, ROLL, steps, units)
    ordered = jax.vmap(lambda held, order: held[order])(hidden, routing)
    ordered = ordered.reshape(N_GROUP, N_GROUP, BLK * steps, units)
    by_section = jnp.swapaxes(ordered, 0, 1).reshape(N_GROUP, N_GROUP * BLK * steps, units)

    def section(triple):
        rows, weight, read = triple
        proj = jnp.dot(rows, weight, preferred_element_type=jnp.float32)
        return jnp.sum(jax.nn.silu(proj) * read[None, :], axis=1)

    score = lax.map(section, (by_section, section_weight, readout))
    score = jnp.swapaxes(score.reshape(N_GROUP, N_GROUP, BLK * steps), 0, 1).reshape(N_GROUP, ROLL, steps)
    placed = jax.vmap(lambda order, vals: jnp.zeros((ROLL, steps), jnp.float32).at[order].set(vals))(routing, score)
    placed = placed.reshape(rollouts, steps)
    live = jnp.arange(steps).astype(jnp.int32)[None, :] < lengths[:, None]
    return jnp.where(live, placed, jnp.float32(0.0))
```

```python
import jax
import jax.numpy as jnp
from jax import lax
from jax.sharding import Mesh, PartitionSpec as P

G = ("xl", "y", "c")
T = ("z", "xh")


def body(acts, gate_weight, up_weight, section_weight, readout, lengths, routing):
    roll, steps, width = acts.shape
    depth, units = gate_weight.shape
    half = units // 2
    core = lax.axis_index("c")
    swap = [(0, 1), (1, 0)]

    def other(x):
        return lax.ppermute(x, "c", swap)

    def in_core_order(own, sister, axis):
        return jnp.where(
            core == 0,
            jnp.concatenate([own, sister], axis),
            jnp.concatenate([sister, own], axis),
        )

    with jax.named_scope("share_weights"):
        low = jnp.concatenate([gate_weight[:, :half], up_weight[:, :half]], 1)
        high = jnp.concatenate([gate_weight[:, half:], up_weight[:, half:]], 1)
        keep = jnp.where(core == 0, low, high)
        give = jnp.where(core == 0, high, low)
        block = in_core_order(keep, other(give), 0)
        weights = lax.all_gather(block, ("xl", "y"), axis=0, tiled=True)
    with jax.named_scope("share_acts"):
        rows = acts.reshape(roll * steps, width)
        sister_rows = other(rows)
        order = routing[0]
        sister_order = other(routing)[0]

    def hidden_of(x, places):
        both = jnp.dot(x, weights, preferred_element_type=jnp.float32)
        h = (jax.nn.silu(both[:, :half]) * both[:, half:]).astype(jnp.bfloat16)
        h = h.reshape(roll, 1, steps, half)
        return h.at[places].get(mode="promise_in_bounds")

    with jax.named_scope("actor"):
        own = hidden_of(rows, order)
        sister = hidden_of(sister_rows, sister_order)
    with jax.named_scope("route"):
        sent = in_core_order(own, sister, 1)
        got = lax.all_to_all(sent, G, split_axis=0, concat_axis=0, tiled=True)
        got = got.reshape(roll // 2, 2, 2 * steps, half)
    with jax.named_scope("section"):
        partial_value = jnp.dot(
            got[:, 0].reshape(-1, half), section_weight[0, :half], preferred_element_type=jnp.float32
        ) + jnp.dot(
            got[:, 1].reshape(-1, half), section_weight[0, half:], preferred_element_type=jnp.float32
        )
        pieces = lax.all_to_all(
            partial_value.reshape(roll, steps, -1), T, split_axis=0, concat_axis=0, tiled=True
        )
        proj = jnp.sum(pieces, axis=0)
        score = jnp.sum(jax.nn.silu(proj) * readout[0][None, :], axis=1)
    with jax.named_scope("back"):
        score = jnp.broadcast_to(score[None, None, :], (roll, 1, steps))
        score = lax.all_to_all(score, T, split_axis=0, concat_axis=0, tiled=True)
        returned = lax.all_to_all(score, G, split_axis=0, concat_axis=0, tiled=True)
        returned = returned.reshape(roll, steps)
        placed = jnp.zeros((roll, steps), jnp.float32).at[order].set(returned)
        live = jnp.arange(steps)[None, :] < lengths[:, None]
        return jnp.where(live, placed, jnp.float32(0.0))


def solution(mesh):
    fine = Mesh(mesh.devices.reshape(2, 8, 2, 8, 4), G + T)
    in_specs = (
        P(G, None, None),
        P(G, T),
        P(G, T),
        P(G, T, None),
        P(G, None),
        P(G),
        P(G, None),
    )
    return jax.shard_map(
        body, mesh=fine, in_specs=in_specs, out_specs=P(G, None), check_vma=False
    )
```

```python
import jax
import jax.numpy as jnp
from jax import lax
from jax.experimental import pallas as pl
from jax.experimental.pallas import tpu as pltpu
from jax.sharding import Mesh, PartitionSpec as P

G = ("xl", "y", "c")
T = ("z", "xh")
LANES = 128
PACK_STEPS = 4
CUT = 144


def pack(order, core, acts):
    roll, steps, width = acts.shape
    blocks = width // (2 * LANES)
    chunk = roll // PACK_STEPS

    def kernel(order_ref, core_ref, acts_ref, keep_ref, give_ref):
        first = pl.program_id(0) * chunk
        mine = core_ref[0] * LANES
        for at in range(chunk):
            source = order_ref[first + at]
            for block in range(blocks):
                to = pl.ds(block * LANES, LANES)
                keep_at = pl.multiple_of(2 * block * LANES + mine, LANES)
                give_at = pl.multiple_of(2 * block * LANES + LANES - mine, LANES)
                keep_ref[at, :, to] = acts_ref[source, :, pl.ds(keep_at, LANES)]
                give_ref[at, :, to] = acts_ref[source, :, pl.ds(give_at, LANES)]

    out = jax.ShapeDtypeStruct((roll, steps, width // 2), acts.dtype)
    return pl.pallas_call(
        kernel,
        grid_spec=pltpu.PrefetchScalarGridSpec(
            num_scalar_prefetch=2,
            grid=(PACK_STEPS,),
            in_specs=[pl.BlockSpec((roll, steps, width), lambda i, o, c: (0, 0, 0))],
            out_specs=[pl.BlockSpec((chunk, steps, width // 2), lambda i, o, c: (i, 0, 0))] * 2,
        ),
        out_shape=[out, out],
        compiler_params=pltpu.CompilerParams(vmem_limit_bytes=32 * 2**20),
    )(order, core, acts)


def project(keep_rows, give_rows, early, late):
    rows, width = keep_rows[0].shape
    sites, _, cut, _ = early.shape
    rest = late.shape[2]
    half = cut + rest
    per = sites // 2
    span = per * LANES
    n = len(keep_rows)
    wide = -(-half // LANES) * LANES

    def kernel(*refs):
        keep_in, give_in = refs[:n], refs[n : 2 * n]
        early_ref, late_ref, keep_out, give_out = refs[2 * n :]
        k = pl.program_id(0)

        @pl.when(k == 0)
        def _():
            keep_out[...] = jnp.zeros_like(keep_out)
            give_out[...] = jnp.zeros_like(give_out)

        for part in range(2):
            piece = jnp.concatenate(
                [
                    jnp.concatenate([early_ref[s, part], late_ref[s, part]], axis=0)
                    for s in range(per)
                ],
                axis=1,
            )
            for ins, out in ((keep_in, keep_out), (give_in, give_out)):
                for at in range(n):
                    out[part, at, :, :half] += lax.dot_general(
                        ins[at][...],
                        piece,
                        (((1,), (1,)), ((), ())),
                        preferred_element_type=jnp.float32,
                    )

    row_spec = pl.BlockSpec((rows, span), lambda k: (0, k))
    out_spec = pl.BlockSpec((2, n, rows, wide), lambda k: (0, 0, 0, 0))
    out = jax.ShapeDtypeStruct((2, n, rows, wide), jnp.float32)
    return pl.pallas_call(
        kernel,
        grid=(4,),
        in_specs=[row_spec] * (2 * n)
        + [
            pl.BlockSpec((per, 2, cut, LANES), lambda k: (k % 2, k // 2, 0, 0)),
            pl.BlockSpec((per, 2, rest, LANES), lambda k: (k % 2, k // 2, 0, 0)),
        ],
        out_specs=[out_spec] * 2,
        out_shape=[out, out],
        compiler_params=pltpu.CompilerParams(vmem_limit_bytes=48 * 2**20),
        cost_estimate=pl.CostEstimate(
            flops=8 * n * rows * width * half, bytes_accessed=12 * 2**20, transcendentals=0
        ),
    )(*keep_rows, *give_rows, early, late)


def activate(side, kept, given, roll, half):
    _, n, rows, wide = kept.shape
    steps = rows // roll

    def kernel(side_ref, kept_ref, given_ref, out_ref):
        gate = kept_ref[0, 0] + given_ref[0, 0]
        up = kept_ref[1, 0] + given_ref[1, 0]
        hidden = (gate * jax.nn.sigmoid(gate) * up)[:, :half]
        out_ref[:, 0] = hidden.reshape(roll, steps, half).astype(out_ref.dtype)

    spec = pl.BlockSpec((2, 1, rows, wide), lambda k, s: (0, k, 0, 0))
    return pl.pallas_call(
        kernel,
        grid_spec=pltpu.PrefetchScalarGridSpec(
            num_scalar_prefetch=1,
            grid=(n,),
            in_specs=[spec, spec],
            out_specs=pl.BlockSpec(
                (roll, 1, steps, half), lambda k, s: (0, k + s[0] - 2 * k * s[0], 0, 0)
            ),
        ),
        out_shape=jax.ShapeDtypeStruct((roll, n, steps, half), jnp.bfloat16),
        compiler_params=pltpu.CompilerParams(vmem_limit_bytes=32 * 2**20),
    )(side, kept, given)


def body(acts, gate_weight, up_weight, section_weight, readout, lengths, routing):
    roll, steps, width = acts.shape
    units = gate_weight.shape[1]
    half = units // 2
    core, side = lax.axis_index("c"), lax.axis_index("xl")
    far = lax.axis_size("xh")
    swap = [(0, 1), (1, 0)]
    order = routing[0]

    with jax.named_scope("share_acts"):
        keep, give = pack(order, core.reshape(1), acts)
        keep = keep.reshape(roll * steps, -1)
        give = give.reshape(roll * steps, -1)
        around = []
        for h in range(far):
            for c in range(2):
                around.append(((0 * 2 + c) * far + h, (1 * 2 + 1 - c) * far + (h - 1) % far))
                around.append(((1 * 2 + c) * far + h, (0 * 2 + 1 - c) * far + (h + 1) % far))
        cross_same = lax.ppermute(keep, "xl", swap)
        cross_other = lax.ppermute(give, ("xl", "c", "xh"), around)
        sister = lax.ppermute(give, "c", swap)
    with jax.named_scope("share_weights"):
        columns = jnp.stack([gate_weight.T, up_weight.T]).reshape(2, 2, half, -1)
        left, right = columns[:, 0], columns[:, 1]
        mine = jnp.where(side == 0, left, right)
        got = lax.ppermute(jnp.where(side == 0, right, left), "xl", swap)
        block = jnp.where(
            side == 0, jnp.concatenate([mine, got], 0), jnp.concatenate([got, mine], 0)
        )
        early = lax.all_gather(block[:, :CUT], "y", axis=0)
        late = lax.all_gather(block[:, CUT:], "y", axis=0)
    with jax.named_scope("actor"):
        kept, given = project([keep, cross_same], [sister, cross_other], early, late)
        given = lax.ppermute(given, "c", swap)
        hidden = activate(side.reshape(1), kept, given, roll, half)
    with jax.named_scope("route"):
        got = lax.all_to_all(hidden, G, split_axis=0, concat_axis=0, tiled=True)
        got = got.reshape(2, roll * steps, half)
    with jax.named_scope("section"):
        partial_value = jnp.dot(
            got[0], section_weight[0, :half], preferred_element_type=jnp.float32
        ) + jnp.dot(got[1], section_weight[0, half:], preferred_element_type=jnp.float32)
        pieces = lax.all_to_all(
            partial_value.reshape(roll, steps, -1), T, split_axis=0, concat_axis=0, tiled=True
        )
        proj = jnp.sum(pieces, axis=0)
        score = jnp.sum(jax.nn.silu(proj) * readout[0][None, :], axis=1)
    with jax.named_scope("back"):
        score = lax.optimization_barrier(jnp.broadcast_to(score[:, None], (steps, LANES)))
        score = lax.optimization_barrier(lax.all_gather(score, T, axis=0))[:, :, 0]
        score = score.reshape(-1, 2, 2, steps).transpose(2, 0, 1, 3).reshape(roll, steps)
        returned = lax.all_to_all(score, G, split_axis=0, concat_axis=0, tiled=True)
        placed = jnp.zeros((roll, steps), jnp.float32).at[order].set(returned)
        live = jnp.arange(steps)[None, :] < lengths[:, None]
        return jnp.where(live, placed, jnp.float32(0.0))


def solution(mesh):
    fine = Mesh(mesh.devices.reshape(2, 8, 2, 8, 4), G + T)
    in_specs = (
        P(G, None, None),
        P(G, T),
        P(G, T),
        P(G, T, None),
        P(G, None),
        P(G),
        P(G, None),
    )
    return jax.shard_map(
        body, mesh=fine, in_specs=in_specs, out_specs=P(G, None), check_vma=False
    )
```

```python
import jax
import jax.numpy as jnp
from jax import lax
from jax.experimental import pallas as pl
from jax.experimental.pallas import tpu as pltpu
from jax.sharding import Mesh, PartitionSpec as P

G = ("xl", "y", "c")
T = ("z", "xh")
LANES = 128
PACK_STEPS = 4
MORE = 32


def pack(order, core, acts):
    roll, steps, width = acts.shape
    blocks = width // (2 * LANES)
    chunk = roll // PACK_STEPS

    def kernel(order_ref, core_ref, acts_ref, keep_ref, give_ref):
        first = pl.program_id(0) * chunk
        mine = core_ref[0] * LANES
        for at in range(chunk):
            source = order_ref[first + at]
            for block in range(blocks):
                to = pl.ds(block * LANES, LANES)
                keep_at = pl.multiple_of(2 * block * LANES + mine, LANES)
                give_at = pl.multiple_of(2 * block * LANES + LANES - mine, LANES)
                keep_ref[at, :, to] = acts_ref[source, :, pl.ds(keep_at, LANES)]
                give_ref[at, :, to] = acts_ref[source, :, pl.ds(give_at, LANES)]

    out = jax.ShapeDtypeStruct((roll, steps, width // 2), acts.dtype)
    return pl.pallas_call(
        kernel,
        grid_spec=pltpu.PrefetchScalarGridSpec(
            num_scalar_prefetch=2,
            grid=(PACK_STEPS,),
            in_specs=[pl.BlockSpec((roll, steps, width), lambda i, o, c: (0, 0, 0))],
            out_specs=[pl.BlockSpec((chunk, steps, width // 2), lambda i, o, c: (i, 0, 0))] * 2,
        ),
        out_shape=[out, out],
        compiler_params=pltpu.CompilerParams(vmem_limit_bytes=32 * 2**20),
    )(order, core, acts)


def project(side, keep_rows, give_rows, near, far):
    rows, width = keep_rows[0].shape
    sites, _, half, _ = far.shape
    n = len(keep_rows)
    span = width // 2
    wide = -(-half // LANES) * LANES

    def kernel(side_ref, *refs):
        ins, weights, outs = refs[: 2 * n], refs[2 * n : 2 * n + 2], refs[2 * n + 2 : 2 * n + 4]
        rows_at, held, row_sem, held_sem = refs[2 * n + 4 :]
        row_copies = [
            pltpu.make_async_copy(ins[at], rows_at.at[at], row_sem.at[at]) for at in range(2 * n)
        ]
        held_copies = [
            pltpu.make_async_copy(
                weights[at].at[site, part, pl.ds(0, half), :],
                held.at[at, part, :, pl.ds(site * LANES, LANES)],
                held_sem.at[at, site, part],
            )
            for at in range(2)
            for site in range(sites)
            for part in range(2)
        ]
        row_copies[0].start()
        for copy in held_copies + row_copies[1:]:
            copy.start()
        for copy in row_copies[:1] + held_copies:
            copy.wait()
        near_at = pl.multiple_of(side_ref[0] * span, span)
        far_at = pl.multiple_of((1 - side_ref[0]) * span, span)
        for at in range(2 * n):
            if at:
                row_copies[at].wait()
            for part in range(2):
                value = lax.dot_general(
                    rows_at[at, :, pl.ds(near_at, span)],
                    held[0, part],
                    (((1,), (1,)), ((), ())),
                    preferred_element_type=jnp.float32,
                ) + lax.dot_general(
                    rows_at[at, :, pl.ds(far_at, span)],
                    held[1, part],
                    (((1,), (1,)), ((), ())),
                    preferred_element_type=jnp.float32,
                )
                outs[at // n][part, at % n, :, :half] = value
                outs[at // n][part, at % n, :, half:] = jnp.zeros((rows, wide - half), jnp.float32)

    held_in = pl.BlockSpec(memory_space=pl.ANY)
    out = jax.ShapeDtypeStruct((2, n, rows, wide), jnp.float32)
    return pl.pallas_call(
        kernel,
        in_specs=[pl.BlockSpec(memory_space=pltpu.SMEM)] + [held_in] * (2 * n + 2),
        out_specs=[pl.BlockSpec(memory_space=pltpu.VMEM)] * 2,
        out_shape=[out, out],
        scratch_shapes=[
            pltpu.VMEM((2 * n, rows, width), far.dtype),
            pltpu.VMEM((2, 2, half, span), far.dtype),
            pltpu.SemaphoreType.DMA((2 * n,)),
            pltpu.SemaphoreType.DMA((2, sites, 2)),
        ],
        compiler_params=pltpu.CompilerParams(vmem_limit_bytes=24 * 2**20),
        cost_estimate=pl.CostEstimate(
            flops=8 * n * rows * width * half, bytes_accessed=10 * 2**20, transcendentals=0
        ),
    )(side, *keep_rows, *give_rows, near, far)


def activate(side, kept, given, roll, half):
    _, n, rows, wide = kept.shape
    steps = rows // roll

    def kernel(side_ref, kept_ref, given_ref, out_ref):
        gate = kept_ref[0, 0] + given_ref[0, 0]
        up = kept_ref[1, 0] + given_ref[1, 0]
        hidden = (gate * jax.nn.sigmoid(gate) * up)[:, :half]
        out_ref[:, 0] = hidden.reshape(roll, steps, half).astype(out_ref.dtype)

    spec = pl.BlockSpec((2, 1, rows, wide), lambda k, s: (0, k, 0, 0))
    return pl.pallas_call(
        kernel,
        grid_spec=pltpu.PrefetchScalarGridSpec(
            num_scalar_prefetch=1,
            grid=(n,),
            in_specs=[spec, spec],
            out_specs=pl.BlockSpec(
                (roll, 1, steps, half), lambda k, s: (0, k + s[0] - 2 * k * s[0], 0, 0)
            ),
        ),
        out_shape=jax.ShapeDtypeStruct((roll, n, steps, half), jnp.bfloat16),
        compiler_params=pltpu.CompilerParams(vmem_limit_bytes=32 * 2**20),
    )(side, kept, given)


def around_x(far):
    pairs = []
    for h in range(far):
        for c in range(2):
            pairs.append(((0 * 2 + c) * far + h, (1 * 2 + 1 - c) * far + (h - 1) % far))
            pairs.append(((1 * 2 + c) * far + h, (0 * 2 + 1 - c) * far + (h + 1) % far))
    return pairs


def front(acts, gate_weight, up_weight, order):
    roll, steps, width = acts.shape
    half = gate_weight.shape[1] // 2
    core, side = lax.axis_index("c"), lax.axis_index("xl")
    swap = [(0, 1), (1, 0)]

    with jax.named_scope("share_weights"):
        columns = jnp.stack([gate_weight.T, up_weight.T]).reshape(2, 2, half, -1)
        left, right = columns[:, 0], columns[:, 1]
        mine = jnp.where(side == 0, left, right)
        got = lax.ppermute(jnp.where(side == 0, right, left), "xl", swap)
    with jax.named_scope("share_acts"):
        keep, give = pack(order, core.reshape(1), acts)
        keep, give, got = lax.optimization_barrier((keep, give, got))
        keep = keep.reshape(roll * steps, -1)
        give = give.reshape(roll * steps, -1)
    with jax.named_scope("share_weights"):
        near = lax.all_gather(jnp.pad(mine, ((0, 0), (0, MORE), (0, 0))), "y", axis=0)
    with jax.named_scope("share_acts"):
        cross_same = lax.ppermute(keep, "xl", swap)
        cross_other = lax.ppermute(give, ("xl", "c", "xh"), around_x(lax.axis_size("xh")))
        sister = lax.ppermute(give, "c", swap)
    with jax.named_scope("share_weights"):
        far = lax.all_gather(got, "y", axis=0)
    with jax.named_scope("actor"):
        at_side = side.reshape(1)
        kept, given = project(at_side, [keep, cross_same], [sister, cross_other], near, far)
        given = lax.ppermute(given, "c", swap)
        return activate(at_side, kept, given, roll, half)


def body(acts, gate_weight, up_weight, section_weight, readout, lengths, routing):
    roll, steps, _ = acts.shape
    half = gate_weight.shape[1] // 2
    order = routing[0]
    hidden = front(acts, gate_weight, up_weight, order)
    with jax.named_scope("route"):
        got = lax.all_to_all(hidden, G, split_axis=0, concat_axis=0, tiled=True)
        got = got.reshape(2, roll * steps, half)
    with jax.named_scope("section"):
        partial_value = jnp.dot(
            got[0], section_weight[0, :half], preferred_element_type=jnp.float32
        ) + jnp.dot(got[1], section_weight[0, half:], preferred_element_type=jnp.float32)
        pieces = lax.all_to_all(
            partial_value.reshape(roll, steps, -1), T, split_axis=0, concat_axis=0, tiled=True
        )
        proj = jnp.sum(pieces, axis=0)
        score = jnp.sum(jax.nn.silu(proj) * readout[0][None, :], axis=1)
    with jax.named_scope("back"):
        score = jnp.broadcast_to(score[None, None, :], (roll, 1, steps))
        score = lax.all_to_all(score, G, split_axis=0, concat_axis=0, tiled=True)
        pairs = []
        for g in range(roll):
            row = (g // 2 % 8) * 4 + g % 2 * 2 + g // 16
            pairs += [(t * roll + row, g * roll + t) for t in range(roll)]
        returned = lax.ppermute(score, G + T, pairs).reshape(roll, steps)
        placed = jnp.zeros((roll, steps), jnp.float32).at[order].set(returned)
        live = jnp.arange(steps)[None, :] < lengths[:, None]
        return jnp.where(live, placed, jnp.float32(0.0))


def solution(mesh):
    fine = Mesh(mesh.devices.reshape(2, 8, 2, 8, 4), G + T)
    in_specs = (
        P(G, None, None),
        P(G, T),
        P(G, T),
        P(G, T, None),
        P(G, None),
        P(G),
        P(G, None),
    )
    return jax.shard_map(
        body, mesh=fine, in_specs=in_specs, out_specs=P(G, None), check_vma=False
    )
```

```python
import jax
import jax.numpy as jnp
from jax import lax
from jax.experimental import pallas as pl
from jax.experimental.pallas import tpu as pltpu
from jax.sharding import Mesh, PartitionSpec as P

G = ("xl", "y", "c")
T = ("z", "xh")
LANES = 128
PACK_STEPS = 4
MORE = 32


def pack(order, core, acts):
    roll, steps, width = acts.shape
    blocks = width // (2 * LANES)
    chunk = roll // PACK_STEPS

    def kernel(order_ref, core_ref, acts_ref, keep_ref, give_ref):
        first = pl.program_id(0) * chunk
        mine = core_ref[0] * LANES
        for at in range(chunk):
            source = order_ref[first + at]
            for block in range(blocks):
                to = pl.ds(block * LANES, LANES)
                keep_at = pl.multiple_of(2 * block * LANES + mine, LANES)
                give_at = pl.multiple_of(2 * block * LANES + LANES - mine, LANES)
                keep_ref[at, :, to] = acts_ref[source, :, pl.ds(keep_at, LANES)]
                give_ref[at, :, to] = acts_ref[source, :, pl.ds(give_at, LANES)]

    out = jax.ShapeDtypeStruct((roll, steps, width // 2), acts.dtype)
    return pl.pallas_call(
        kernel,
        grid_spec=pltpu.PrefetchScalarGridSpec(
            num_scalar_prefetch=2,
            grid=(PACK_STEPS,),
            in_specs=[pl.BlockSpec((roll, steps, width), lambda i, o, c: (0, 0, 0))],
            out_specs=[pl.BlockSpec((chunk, steps, width // 2), lambda i, o, c: (i, 0, 0))] * 2,
        ),
        out_shape=[out, out],
        compiler_params=pltpu.CompilerParams(vmem_limit_bytes=32 * 2**20),
    )(order, core, acts)


def project(side, keep_rows, give_rows, near, far):
    rows, width = keep_rows[0].shape
    sites, _, half, _ = far.shape
    n = len(keep_rows)
    span = width // 2
    wide = -(-half // LANES) * LANES

    def kernel(side_ref, *refs):
        ins, weights, outs = refs[: 2 * n], refs[2 * n : 2 * n + 2], refs[2 * n + 2 : 2 * n + 4]
        rows_at, held, row_sem, held_sem = refs[2 * n + 4 :]
        row_copies = [
            pltpu.make_async_copy(ins[at], rows_at.at[at], row_sem.at[at]) for at in range(2 * n)
        ]
        held_copies = [
            pltpu.make_async_copy(
                weights[at].at[site, part, pl.ds(0, half), :],
                held.at[at, part, :, pl.ds(site * LANES, LANES)],
                held_sem.at[at, site, part],
            )
            for at in range(2)
            for site in range(sites)
            for part in range(2)
        ]
        row_copies[0].start()
        for copy in held_copies + row_copies[1:]:
            copy.start()
        for copy in row_copies[:1] + held_copies:
            copy.wait()
        near_at = pl.multiple_of(side_ref[0] * span, span)
        far_at = pl.multiple_of((1 - side_ref[0]) * span, span)
        for at in range(2 * n):
            if at:
                row_copies[at].wait()
            for part in range(2):
                value = lax.dot_general(
                    rows_at[at, :, pl.ds(near_at, span)],
                    held[0, part],
                    (((1,), (1,)), ((), ())),
                    preferred_element_type=jnp.float32,
                ) + lax.dot_general(
                    rows_at[at, :, pl.ds(far_at, span)],
                    held[1, part],
                    (((1,), (1,)), ((), ())),
                    preferred_element_type=jnp.float32,
                )
                outs[at // n][part, at % n, :, :half] = value
                outs[at // n][part, at % n, :, half:] = jnp.zeros((rows, wide - half), jnp.float32)

    held_in = pl.BlockSpec(memory_space=pltpu.HBM)
    out = jax.ShapeDtypeStruct((2, n, rows, wide), jnp.float32)
    return pl.pallas_call(
        kernel,
        in_specs=[pl.BlockSpec(memory_space=pltpu.SMEM)] + [held_in] * (2 * n + 2),
        out_specs=[pl.BlockSpec(memory_space=pltpu.VMEM)] * 2,
        out_shape=[out, out],
        scratch_shapes=[
            pltpu.VMEM((2 * n, rows, width), far.dtype),
            pltpu.VMEM((2, 2, half, span), far.dtype),
            pltpu.SemaphoreType.DMA((2 * n,)),
            pltpu.SemaphoreType.DMA((2, sites, 2)),
        ],
        cost_estimate=pl.CostEstimate(
            flops=8 * n * rows * width * half, bytes_accessed=10 * 2**20, transcendentals=0
        ),
    )(side, *keep_rows, *give_rows, near, far)


def activate(side, kept, given, roll, half):
    _, n, rows, wide = kept.shape
    steps = rows // roll

    def kernel(side_ref, kept_ref, given_ref, out_ref):
        gate = kept_ref[0, 0] + given_ref[0, 0]
        up = kept_ref[1, 0] + given_ref[1, 0]
        hidden = (gate * jax.nn.sigmoid(gate) * up)[:, :half]
        out_ref[:, 0] = hidden.reshape(roll, steps, half).astype(out_ref.dtype)

    spec = pl.BlockSpec((2, 1, rows, wide), lambda k, s: (0, k, 0, 0))
    return pl.pallas_call(
        kernel,
        grid_spec=pltpu.PrefetchScalarGridSpec(
            num_scalar_prefetch=1,
            grid=(n,),
            in_specs=[spec, spec],
            out_specs=pl.BlockSpec(
                (roll, 1, steps, half), lambda k, s: (0, k + s[0] - 2 * k * s[0], 0, 0)
            ),
        ),
        out_shape=jax.ShapeDtypeStruct((roll, n, steps, half), jnp.bfloat16),
    )(side, kept, given)


def around_x(far):
    pairs = []
    for h in range(far):
        for c in range(2):
            pairs.append(((0 * 2 + c) * far + h, (1 * 2 + 1 - c) * far + (h - 1) % far))
            pairs.append(((1 * 2 + c) * far + h, (0 * 2 + 1 - c) * far + (h + 1) % far))
    return pairs


def front(acts, gate_weight, up_weight, order):
    roll, steps, width = acts.shape
    half = gate_weight.shape[1] // 2
    core, side = lax.axis_index("c"), lax.axis_index("xl")
    swap = [(0, 1), (1, 0)]

    with jax.named_scope("share_weights"):
        columns = jnp.stack([gate_weight.T, up_weight.T]).reshape(2, 2, half, -1)
        left, right = columns[:, 0], columns[:, 1]
        padded = jnp.pad(columns, ((0, 0), (0, 0), (0, MORE), (0, 0)))
        mine = jnp.where(side == 0, padded[:, 0], padded[:, 1])
        got = lax.ppermute(jnp.where(side == 0, right, left), "xl", swap)
    with jax.named_scope("share_acts"):
        keep, give = pack(order, core.reshape(1), acts)
        keep, give, got = lax.optimization_barrier((keep, give, got))
        keep = keep.reshape(roll * steps, -1)
        give = give.reshape(roll * steps, -1)
    with jax.named_scope("share_weights"):
        near = lax.all_gather(mine, "y", axis=0)
    with jax.named_scope("share_acts"):
        cross_same = lax.ppermute(keep, "xl", swap)
        cross_other = lax.ppermute(give, ("xl", "c", "xh"), around_x(lax.axis_size("xh")))
        sister = lax.ppermute(give, "c", swap)
    with jax.named_scope("share_weights"):
        far = lax.all_gather(got, "y", axis=0)
    with jax.named_scope("actor"):
        at_side = side.reshape(1)
        kept, given = project(at_side, [keep, cross_same], [sister, cross_other], near, far)
        given = lax.ppermute(given, "c", swap)
        return activate(at_side, kept, given, roll, half)


def body(acts, gate_weight, up_weight, section_weight, readout, lengths, routing):
    roll, steps, _ = acts.shape
    half = gate_weight.shape[1] // 2
    order = routing[0]
    hidden = front(acts, gate_weight, up_weight, order)
    with jax.named_scope("route"):
        got = lax.all_to_all(hidden, G, split_axis=0, concat_axis=0, tiled=True)
        got = got.reshape(2, roll * steps, half)
    with jax.named_scope("section"):
        partial_value = jnp.dot(
            got[0], section_weight[0, :half], preferred_element_type=jnp.float32
        ) + jnp.dot(got[1], section_weight[0, half:], preferred_element_type=jnp.float32)
        partial_value = partial_value.astype(jnp.bfloat16).reshape(roll, steps, -1)
        pieces = lax.all_to_all(partial_value, T, split_axis=0, concat_axis=0, tiled=True)
        proj = jnp.sum(pieces.astype(jnp.float32), axis=0)
        score = jnp.sum(jax.nn.silu(proj) * readout[0][None, :], axis=1)
    with jax.named_scope("back"):
        score = jnp.broadcast_to(score[None, None, :], (roll, 1, steps))
        score = lax.all_to_all(score, G, split_axis=0, concat_axis=0, tiled=True)
        pairs = []
        for g in range(roll):
            row = (g // 2 % 8) * 4 + g % 2 * 2 + g // 16
            pairs += [(t * roll + row, g * roll + t) for t in range(roll)]
        returned = lax.ppermute(score, G + T, pairs).reshape(roll, steps)
        here = order[:, None, None] == jnp.arange(roll)[None, None, :]
        placed = jnp.sum(jnp.where(here, returned[:, :, None], 0.0), axis=0)
        live = jnp.arange(steps)[:, None] < lengths[None, :]
        return jnp.where(live, placed, jnp.float32(0.0)).T


def solution(mesh):
    fine = Mesh(mesh.devices.reshape(2, 8, 2, 8, 4), G + T)
    in_specs = (
        P(G, None, None),
        P(G, T),
        P(G, T),
        P(G, T, None),
        P(G, None),
        P(G),
        P(G, None),
    )
    return jax.shard_map(
        body, mesh=fine, in_specs=in_specs, out_specs=P(G, None), check_vma=False
    )
```

```python
import jax
import jax.numpy as jnp
from jax import lax
from jax.experimental import pallas as pl
from jax.experimental.pallas import tpu as pltpu
from jax.sharding import Mesh, PartitionSpec as P

G = ("xl", "y", "c")
T = ("z", "xh")
LANES = 128
MORE = 32


def pack(routing, core, acts):
    roll, steps, width = acts.shape
    blocks = width // (2 * LANES)

    def kernel(routing_ref, core_ref, acts_ref, keep_ref, give_ref, rows, sem):
        copies = [
            pltpu.make_async_copy(acts_ref.at[routing_ref[0, at]], rows.at[at], sem.at[at])
            for at in range(roll)
        ]
        for copy in copies:
            copy.start()
        mine = core_ref[0] * LANES
        for at in range(roll):
            copies[at].wait()
            for block in range(blocks):
                to = pl.ds(block * LANES, LANES)
                keep_at = pl.multiple_of(2 * block * LANES + mine, LANES)
                give_at = pl.multiple_of(2 * block * LANES + LANES - mine, LANES)
                keep_ref[at, :, to] = rows[at, :, pl.ds(keep_at, LANES)]
                give_ref[at, :, to] = rows[at, :, pl.ds(give_at, LANES)]

    smem, vmem = pl.BlockSpec(memory_space=pltpu.SMEM), pl.BlockSpec(memory_space=pltpu.VMEM)
    out = jax.ShapeDtypeStruct((roll, steps, width // 2), acts.dtype)
    return pl.pallas_call(
        kernel,
        in_specs=[smem, smem, pl.BlockSpec(memory_space=pl.ANY)],
        out_specs=[vmem, vmem],
        out_shape=[out, out],
        scratch_shapes=[pltpu.VMEM(acts.shape, acts.dtype), pltpu.SemaphoreType.DMA((roll,))],
    )(routing, core, acts)


def project(side, rows_in, near, far):
    rows, width = rows_in[0].shape
    sites, _, half, _ = far.shape
    n = len(rows_in)
    span = width // 2
    wide = -(-half // LANES) * LANES

    def kernel(side_ref, *refs):
        ins, weights, out = refs[:n], refs[n : n + 2], refs[n + 2]
        rows_at, held, row_sem, held_sem = refs[n + 3 :]
        near_first = pl.multiple_of(side_ref[0] * MORE, MORE)
        copies = [
            pltpu.make_async_copy(
                ins[at], rows_at.at[pl.ds(at * rows, rows)], row_sem.at[at]
            )
            for at in range(n)
        ] + [
            pltpu.make_async_copy(
                weights[at].at[site, part, pl.ds(near_first if at == 0 else 0, half), :],
                held.at[at, part, :, pl.ds(site * LANES, LANES)],
                held_sem.at[at, site, part],
            )
            for at in range(2)
            for site in range(sites)
            for part in range(2)
        ]
        for copy in copies:
            copy.start()
        for copy in copies:
            copy.wait()
        near_at = pl.multiple_of(side_ref[0] * span, span)
        far_at = pl.multiple_of((1 - side_ref[0]) * span, span)
        for part in range(2):
            value = lax.dot_general(
                rows_at[:, pl.ds(near_at, span)],
                held[0, part],
                (((1,), (1,)), ((), ())),
                preferred_element_type=jnp.float32,
            ) + lax.dot_general(
                rows_at[:, pl.ds(far_at, span)],
                held[1, part],
                (((1,), (1,)), ((), ())),
                preferred_element_type=jnp.float32,
            )
            out[part, :, :, :half] = value.reshape(n, rows, half)
            out[part, :, :, half:] = jnp.zeros((n, rows, wide - half), jnp.float32)

    in_place = pl.BlockSpec(memory_space=pl.ANY)
    return pl.pallas_call(
        kernel,
        in_specs=[pl.BlockSpec(memory_space=pltpu.SMEM)] + [in_place] * (n + 2),
        out_specs=pl.BlockSpec(memory_space=pltpu.VMEM),
        out_shape=jax.ShapeDtypeStruct((2, n, rows, wide), jnp.float32),
        scratch_shapes=[
            pltpu.VMEM((n * rows, width), far.dtype),
            pltpu.VMEM((2, 2, half, span), far.dtype),
            pltpu.SemaphoreType.DMA((n,)),
            pltpu.SemaphoreType.DMA((2, sites, 2)),
        ],
        compiler_params=pltpu.CompilerParams(vmem_limit_bytes=16 * 2**20),
        cost_estimate=pl.CostEstimate(
            flops=4 * n * rows * width * half, bytes_accessed=5 * 2**20, transcendentals=0
        ),
    )(side, *rows_in, near, far)


def activate(side, kept, given, roll, half):
    _, n, rows, wide = kept.shape
    steps = rows // roll

    def kernel(side_ref, kept_ref, given_ref, out_ref):
        gate = kept_ref[0, 0] + given_ref[0, 0]
        up = kept_ref[1, 0] + given_ref[1, 0]
        hidden = (gate * jax.nn.sigmoid(gate) * up)[:, :half]
        out_ref[:, 0] = hidden.reshape(roll, steps, half).astype(out_ref.dtype)

    spec = pl.BlockSpec((2, 1, rows, wide), lambda k, s: (0, k, 0, 0))
    return pl.pallas_call(
        kernel,
        grid_spec=pltpu.PrefetchScalarGridSpec(
            num_scalar_prefetch=1,
            grid=(n,),
            in_specs=[spec, spec],
            out_specs=pl.BlockSpec(
                (roll, 1, steps, half), lambda k, s: (0, k + s[0] - 2 * k * s[0], 0, 0)
            ),
        ),
        out_shape=jax.ShapeDtypeStruct((roll, n, steps, half), jnp.bfloat16),
        compiler_params=pltpu.CompilerParams(vmem_limit_bytes=16 * 2**20),
    )(side, kept, given)


def around_x(far):
    pairs = []
    for h in range(far):
        for c in range(2):
            pairs.append(((0 * 2 + c) * far + h, (1 * 2 + 1 - c) * far + (h - 1) % far))
            pairs.append(((1 * 2 + c) * far + h, (0 * 2 + 1 - c) * far + (h + 1) % far))
    return pairs


def front(acts, gate_weight, up_weight, routing):
    roll, steps, width = acts.shape
    half = gate_weight.shape[1] // 2
    core, side = lax.axis_index("c"), lax.axis_index("xl")
    swap = [(0, 1), (1, 0)]

    with jax.named_scope("share_weights"):
        gate_t, up_t = gate_weight.T, up_weight.T

        def columns(first, count):
            return jnp.stack(
                [lax.dynamic_slice_in_dim(w, first, count, 0) for w in (gate_t, up_t)]
            )

        mine = columns(side * (half - MORE), half + MORE)
        got = lax.ppermute(columns((1 - side) * half, half), "xl", swap)
    with jax.named_scope("share_acts"):
        keep, give = pack(routing, core.reshape(1), acts)
        keep, give, got = lax.optimization_barrier((keep, give, got))
        keep = keep.reshape(roll * steps, -1)
        give = give.reshape(roll * steps, -1)
    with jax.named_scope("share_weights"):
        near = lax.all_gather(mine, "y", axis=0)
    with jax.named_scope("share_acts"):
        cross_same = lax.ppermute(keep, "xl", swap)
        cross_other = lax.ppermute(give, ("xl", "c", "xh"), around_x(lax.axis_size("xh")))
        sister = lax.ppermute(give, "c", swap)
    with jax.named_scope("share_weights"):
        far = lax.all_gather(got, "y", axis=0)
    with jax.named_scope("actor"):
        at_side = side.reshape(1)
        given = project(at_side, [sister, cross_other], near, far)
        given = lax.ppermute(given, "c", swap)
        kept = project(at_side, [keep, cross_same], near, far)
        return activate(at_side, kept, given, roll, half)


def body(acts, gate_weight, up_weight, section_weight, readout, lengths, routing):
    roll, steps, _ = acts.shape
    half = gate_weight.shape[1] // 2
    order = routing[0]
    hidden = front(acts, gate_weight, up_weight, routing)
    with jax.named_scope("route"):
        got = lax.all_to_all(hidden, G, split_axis=0, concat_axis=0, tiled=True)
        got = got.reshape(2, roll * steps, half)
    with jax.named_scope("section"):
        partial_value = jnp.dot(
            got[0], section_weight[0, :half], preferred_element_type=jnp.float32
        ) + jnp.dot(got[1], section_weight[0, half:], preferred_element_type=jnp.float32)
        partial_value = partial_value.astype(jnp.bfloat16).reshape(roll, steps, -1)
        pieces = lax.all_to_all(partial_value, T, split_axis=0, concat_axis=0, tiled=True)
        proj = jnp.sum(pieces.astype(jnp.float32), axis=0)
        score = jnp.sum(jax.nn.silu(proj) * readout[0][None, :], axis=1)
    with jax.named_scope("back"):
        score = jnp.broadcast_to(score[None, None, :], (roll, 1, steps))
        score = lax.all_to_all(score, G, split_axis=0, concat_axis=0, tiled=True)
        pairs = []
        for g in range(roll):
            row = (g // 2 % 8) * 4 + g % 2 * 2 + g // 16
            pairs += [(t * roll + row, g * roll + t) for t in range(roll)]
        returned = lax.ppermute(score, G + T, pairs).reshape(roll, steps)
        here = order[:, None, None] == jnp.arange(roll)[None, None, :]
        placed = jnp.sum(jnp.where(here, returned[:, :, None], 0.0), axis=0)
        live = jnp.arange(steps)[:, None] < lengths[None, :]
        return jnp.where(live, placed, jnp.float32(0.0)).T


def solution(mesh):
    fine = Mesh(mesh.devices.reshape(2, 8, 2, 8, 4), G + T)
    in_specs = (
        P(G, None, None),
        P(G, T),
        P(G, T),
        P(G, T, None),
        P(G, None),
        P(G),
        P(G, None),
    )
    return jax.shard_map(
        body, mesh=fine, in_specs=in_specs, out_specs=P(G, None), check_vma=False
    )
```

```python
import jax
import jax.numpy as jnp
from jax import lax
from jax.experimental import pallas as pl
from jax.experimental.pallas import tpu as pltpu
from jax.sharding import Mesh, PartitionSpec as P

G = ("xl", "y", "c")
T = ("z", "xh")
LANES = 128
MORE = 32
FIRST = 50
SECOND = 16


def pack(routing, core, acts):
    roll, steps, width = acts.shape
    blocks = width // (2 * LANES)

    def kernel(routing_ref, core_ref, acts_ref, keep_ref, give_ref, rows, sem):
        copies = [
            pltpu.make_async_copy(acts_ref.at[routing_ref[0, at]], rows.at[at], sem.at[at])
            for at in range(roll)
        ]
        for copy in copies:
            copy.start()
        mine = core_ref[0] * LANES
        for at in range(roll):
            copies[at].wait()
            for block in range(blocks):
                to = pl.ds(block * LANES, LANES)
                keep_at = pl.multiple_of(2 * block * LANES + mine, LANES)
                give_at = pl.multiple_of(2 * block * LANES + LANES - mine, LANES)
                keep_ref[at, :, to] = rows[at, :, pl.ds(keep_at, LANES)]
                give_ref[at, :, to] = rows[at, :, pl.ds(give_at, LANES)]

    smem, vmem = pl.BlockSpec(memory_space=pltpu.SMEM), pl.BlockSpec(memory_space=pltpu.VMEM)
    out = jax.ShapeDtypeStruct((roll, steps, width // 2), acts.dtype)
    return pl.pallas_call(
        kernel,
        in_specs=[smem, smem, pl.BlockSpec(memory_space=pl.ANY)],
        out_specs=[vmem, vmem],
        out_shape=[out, out],
        scratch_shapes=[pltpu.VMEM(acts.shape, acts.dtype), pltpu.SemaphoreType.DMA((roll,))],
    )(routing, core, acts)


def project(side, rows_in, near, far, limit):
    rows, width = rows_in[0].shape
    sites, _, half, _ = far.shape
    n = len(rows_in)
    span = width // 2
    wide = -(-half // LANES) * LANES

    def kernel(side_ref, *refs):
        ins, weights, out = refs[:n], refs[n : n + 2], refs[n + 2]
        rows_at, held, row_sem, held_sem = refs[n + 3 :]
        near_first = pl.multiple_of(side_ref[0] * MORE, MORE)
        copies = [
            pltpu.make_async_copy(
                ins[at], rows_at.at[pl.ds(at * rows, rows)], row_sem.at[at]
            )
            for at in range(n)
        ] + [
            pltpu.make_async_copy(
                weights[at].at[site, part, pl.ds(near_first if at == 0 else 0, half), :],
                held.at[at, part, :, pl.ds(site * LANES, LANES)],
                held_sem.at[at, site, part],
            )
            for at in range(2)
            for site in range(sites)
            for part in range(2)
        ]
        for copy in copies:
            copy.start()
        for copy in copies:
            copy.wait()
        near_at = pl.multiple_of(side_ref[0] * span, span)
        far_at = pl.multiple_of((1 - side_ref[0]) * span, span)
        for part in range(2):
            value = lax.dot_general(
                rows_at[:, pl.ds(near_at, span)],
                held[0, part],
                (((1,), (1,)), ((), ())),
                preferred_element_type=jnp.float32,
            ) + lax.dot_general(
                rows_at[:, pl.ds(far_at, span)],
                held[1, part],
                (((1,), (1,)), ((), ())),
                preferred_element_type=jnp.float32,
            )
            out[part, :, :, :half] = value.reshape(n, rows, half)
            out[part, :, :, half:] = jnp.zeros((n, rows, wide - half), jnp.float32)

    in_place = pl.BlockSpec(memory_space=pl.ANY)
    return pl.pallas_call(
        kernel,
        in_specs=[pl.BlockSpec(memory_space=pltpu.SMEM)] + [in_place] * (n + 2),
        out_specs=pl.BlockSpec(memory_space=pltpu.VMEM),
        out_shape=jax.ShapeDtypeStruct((2, n, rows, wide), jnp.float32),
        scratch_shapes=[
            pltpu.VMEM((n * rows, width), far.dtype),
            pltpu.VMEM((2, 2, half, span), far.dtype),
            pltpu.SemaphoreType.DMA((n,)),
            pltpu.SemaphoreType.DMA((2, sites, 2)),
        ],
        compiler_params=pltpu.CompilerParams(vmem_limit_bytes=limit * 2**20),
        cost_estimate=pl.CostEstimate(
            flops=4 * n * rows * width * half, bytes_accessed=5 * 2**20, transcendentals=0
        ),
    )(side, *rows_in, near, far)


def activate(side, kept, given, roll, half):
    _, n, rows, wide = kept.shape
    steps = rows // roll

    def kernel(side_ref, kept_ref, given_ref, out_ref):
        gate = kept_ref[0, 0] + given_ref[0, 0]
        up = kept_ref[1, 0] + given_ref[1, 0]
        hidden = (gate * jax.nn.sigmoid(gate) * up)[:, :half]
        out_ref[:, 0] = hidden.reshape(roll, steps, half).astype(out_ref.dtype)

    spec = pl.BlockSpec((2, 1, rows, wide), lambda k, s: (0, k, 0, 0))
    return pl.pallas_call(
        kernel,
        grid_spec=pltpu.PrefetchScalarGridSpec(
            num_scalar_prefetch=1,
            grid=(n,),
            in_specs=[spec, spec],
            out_specs=pl.BlockSpec(
                (roll, 1, steps, half), lambda k, s: (0, k + s[0] - 2 * k * s[0], 0, 0)
            ),
        ),
        out_shape=jax.ShapeDtypeStruct((roll, n, steps, half), jnp.bfloat16),
        compiler_params=pltpu.CompilerParams(vmem_limit_bytes=16 * 2**20),
    )(side, kept, given)


def around_x(far):
    pairs = []
    for h in range(far):
        for c in range(2):
            pairs.append(((0 * 2 + c) * far + h, (1 * 2 + 1 - c) * far + (h - 1) % far))
            pairs.append(((1 * 2 + c) * far + h, (0 * 2 + 1 - c) * far + (h + 1) % far))
    return pairs


def across(count):
    def hops(a, b):
        return min((a - b) % 8, (b - a) % 8)

    def apart(source, row, g, t):
        along_x = hops(2 * (row % 4) + source // 16, 2 * (t % 4) + g // 16)
        return along_x + hops(source // 2 % 8, g // 2 % 8) + hops(row // 4, t // 4)

    pairs = []
    for g in range(count):
        row = (g // 2 % 8) * 4 + g % 2 * 2 + g // 16
        free = list(range(count))
        for t in sorted(range(count), key=lambda t: -apart(g, row, g, t)):
            source = min(free, key=lambda source: apart(source, row, g, t))
            free.remove(source)
            pairs.append((source * count + row, g * count + t))
    return pairs


def front(acts, gate_weight, up_weight, routing):
    roll, steps, width = acts.shape
    half = gate_weight.shape[1] // 2
    core, side = lax.axis_index("c"), lax.axis_index("xl")
    swap = [(0, 1), (1, 0)]

    with jax.named_scope("share_weights"):
        gate_t, up_t = gate_weight.T, up_weight.T

        def columns(first, count):
            return jnp.stack(
                [lax.dynamic_slice_in_dim(w, first, count, 0) for w in (gate_t, up_t)]
            )

        mine = columns(side * (half - MORE), half + MORE)
        got = lax.ppermute(columns((1 - side) * half, half), "xl", swap)
    with jax.named_scope("share_acts"):
        keep, give = pack(routing, core.reshape(1), acts)
        keep, give, got = lax.optimization_barrier((keep, give, got))
        keep = keep.reshape(roll * steps, -1)
        give = give.reshape(roll * steps, -1)
    with jax.named_scope("share_weights"):
        near = lax.all_gather(mine, "y", axis=0)
    with jax.named_scope("share_acts"):
        cross_same = lax.ppermute(keep, "xl", swap)
        cross_other = lax.ppermute(give, ("xl", "c", "xh"), around_x(lax.axis_size("xh")))
        sister = lax.ppermute(give, "c", swap)
    with jax.named_scope("share_weights"):
        far = lax.all_gather(got, "y", axis=0)
    with jax.named_scope("actor"):
        at_side = side.reshape(1)
        given = project(at_side, [sister, cross_other], near, far, FIRST)
        given = lax.ppermute(given, "c", swap)
        kept = project(at_side, [keep, cross_same], near, far, SECOND)
        return activate(at_side, kept, given, roll, half)


def body(acts, gate_weight, up_weight, section_weight, readout, lengths, routing):
    roll, steps, _ = acts.shape
    half = gate_weight.shape[1] // 2
    order = routing[0]
    hidden = front(acts, gate_weight, up_weight, routing)
    with jax.named_scope("route"):
        got = lax.all_to_all(hidden, G, split_axis=0, concat_axis=0, tiled=True)
        got = got.reshape(2, roll * steps, half)
    with jax.named_scope("section"):
        partial_value = jnp.dot(
            got[0], section_weight[0, :half], preferred_element_type=jnp.float32
        ) + jnp.dot(got[1], section_weight[0, half:], preferred_element_type=jnp.float32)
        partial_value = partial_value.astype(jnp.bfloat16).reshape(roll, steps, -1)
        pieces = lax.all_to_all(partial_value, T, split_axis=0, concat_axis=0, tiled=True)
        proj = jnp.sum(pieces.astype(jnp.float32), axis=0)
        score = jnp.sum(jax.nn.silu(proj) * readout[0][None, :], axis=1)
    with jax.named_scope("back"):
        score = jnp.broadcast_to(score[None, None, :], (roll, 1, steps))
        score = lax.all_to_all(score, G, split_axis=0, concat_axis=0, tiled=True)
        returned = lax.ppermute(score, G + T, across(roll)).reshape(roll, steps)
        here = order[:, None, None] == jnp.arange(roll)[None, None, :]
        placed = jnp.sum(jnp.where(here, returned[:, :, None], 0.0), axis=0)
        live = jnp.arange(steps)[:, None] < lengths[None, :]
        return jnp.where(live, placed, jnp.float32(0.0)).T


def solution(mesh):
    fine = Mesh(mesh.devices.reshape(2, 8, 2, 8, 4), G + T)
    in_specs = (
        P(G, None, None),
        P(G, T),
        P(G, T),
        P(G, T, None),
        P(G, None),
        P(G),
        P(G, None),
    )
    return jax.shard_map(
        body, mesh=fine, in_specs=in_specs, out_specs=P(G, None), check_vma=False
    )
```

```python
import jax
import jax.numpy as jnp
from jax import lax
from jax.experimental import pallas as pl
from jax.experimental.pallas import tpu as pltpu
from jax.sharding import Mesh, PartitionSpec as P

G = ("xl", "y", "c")
T = ("z", "xh")
LANES = 128
MORE = 32
FIRST = 50
SECOND = 16


def pack(routing, core, acts):
    roll, steps, width = acts.shape
    blocks = width // (2 * LANES)

    def kernel(routing_ref, core_ref, acts_ref, keep_ref, give_ref, rows, sem):
        copies = [
            pltpu.make_async_copy(acts_ref.at[routing_ref[0, at]], rows.at[at], sem.at[at])
            for at in range(roll)
        ]
        for copy in copies:
            copy.start()
        mine = core_ref[0] * LANES
        for at in range(roll):
            copies[at].wait()
            for block in range(blocks):
                to = pl.ds(block * LANES, LANES)
                keep_at = pl.multiple_of(2 * block * LANES + mine, LANES)
                give_at = pl.multiple_of(2 * block * LANES + LANES - mine, LANES)
                keep_ref[at, :, to] = rows[at, :, pl.ds(keep_at, LANES)]
                give_ref[at, :, to] = rows[at, :, pl.ds(give_at, LANES)]

    smem, vmem = pl.BlockSpec(memory_space=pltpu.SMEM), pl.BlockSpec(memory_space=pltpu.VMEM)
    out = jax.ShapeDtypeStruct((roll, steps, width // 2), acts.dtype)
    return pl.pallas_call(
        kernel,
        in_specs=[smem, smem, pl.BlockSpec(memory_space=pl.ANY)],
        out_specs=[vmem, vmem],
        out_shape=[out, out],
        scratch_shapes=[pltpu.VMEM(acts.shape, acts.dtype), pltpu.SemaphoreType.DMA((roll,))],
    )(routing, core, acts)


def project(side, rows_in, near, far, limit):
    rows, width = rows_in[0].shape
    sites, _, half, _ = far.shape
    n = len(rows_in)
    span = width // 2
    wide = -(-half // LANES) * LANES

    def kernel(side_ref, *refs):
        ins, weights, out = refs[:n], refs[n : n + 2], refs[n + 2]
        rows_at, weights_at, held, row_sem, weight_sem = refs[n + 3 :]
        near_first = pl.multiple_of(side_ref[0] * MORE, MORE)
        row_copies = [
            pltpu.make_async_copy(
                ins[at], rows_at.at[pl.ds(at * rows, rows)], row_sem.at[at]
            )
            for at in range(n)
        ]
        weight_copies = [
            pltpu.make_async_copy(
                weights[at].at[:, :, pl.ds(near_first if at == 0 else 0, half), :],
                weights_at.at[at],
                weight_sem.at[at],
            )
            for at in range(2)
        ]
        for copy in weight_copies + row_copies:
            copy.start()
        for at in (1, 0):
            weight_copies[at].wait()
            for part in range(2):
                for site in range(sites):
                    to = pl.ds(site * LANES, LANES)
                    held[at, part, :, to] = weights_at[at, site, part]
        for copy in row_copies:
            copy.wait()

        def product(at, part):
            first = side_ref[0] if at == 0 else 1 - side_ref[0]
            return lax.dot_general(
                rows_at[:, pl.ds(pl.multiple_of(first * span, span), span)],
                held[at, part],
                (((1,), (1,)), ((), ())),
                preferred_element_type=jnp.float32,
            )

        for part in range(2):
            value = product(0, part) + product(1, part)
            out[part, :, :, :half] = value.reshape(n, rows, half)
            out[part, :, :, half:] = jnp.zeros((n, rows, wide - half), jnp.float32)

    in_place = pl.BlockSpec(memory_space=pl.ANY)
    return pl.pallas_call(
        kernel,
        in_specs=[pl.BlockSpec(memory_space=pltpu.SMEM)] + [in_place] * (n + 2),
        out_specs=pl.BlockSpec(memory_space=pltpu.VMEM),
        out_shape=jax.ShapeDtypeStruct((2, n, rows, wide), jnp.float32),
        scratch_shapes=[
            pltpu.VMEM((n * rows, width), far.dtype),
            pltpu.VMEM((2, sites, 2, half, LANES), far.dtype),
            pltpu.VMEM((2, 2, half, span), far.dtype),
            pltpu.SemaphoreType.DMA((n,)),
            pltpu.SemaphoreType.DMA((2,)),
        ],
        compiler_params=pltpu.CompilerParams(vmem_limit_bytes=limit * 2**20),
        cost_estimate=pl.CostEstimate(
            flops=4 * n * rows * width * half, bytes_accessed=5 * 2**20, transcendentals=0
        ),
    )(side, *rows_in, near, far)


def activate(side, kept, given, roll, half):
    _, n, rows, wide = kept.shape
    steps = rows // roll

    def kernel(side_ref, kept_ref, given_ref, out_ref):
        gate = kept_ref[0, 0] + given_ref[0, 0]
        up = kept_ref[1, 0] + given_ref[1, 0]
        hidden = (gate * jax.nn.sigmoid(gate) * up)[:, :half]
        out_ref[:, 0] = hidden.reshape(roll, steps, half).astype(out_ref.dtype)

    spec = pl.BlockSpec((2, 1, rows, wide), lambda k, s: (0, k, 0, 0))
    return pl.pallas_call(
        kernel,
        grid_spec=pltpu.PrefetchScalarGridSpec(
            num_scalar_prefetch=1,
            grid=(n,),
            in_specs=[spec, spec],
            out_specs=pl.BlockSpec(
                (roll, 1, steps, half), lambda k, s: (0, k + s[0] - 2 * k * s[0], 0, 0)
            ),
        ),
        out_shape=jax.ShapeDtypeStruct((roll, n, steps, half), jnp.bfloat16),
        compiler_params=pltpu.CompilerParams(vmem_limit_bytes=16 * 2**20),
    )(side, kept, given)


def around_x(far):
    pairs = []
    for h in range(far):
        for c in range(2):
            pairs.append(((0 * 2 + c) * far + h, (1 * 2 + 1 - c) * far + (h - 1) % far))
            pairs.append(((1 * 2 + c) * far + h, (0 * 2 + 1 - c) * far + (h + 1) % far))
    return pairs


def across(count):
    def hops(a, b):
        return min((a - b) % 8, (b - a) % 8)

    def apart(source, row, g, t):
        along_x = hops(2 * (row % 4) + source // 16, 2 * (t % 4) + g // 16)
        return along_x + hops(source // 2 % 8, g // 2 % 8) + hops(row // 4, t // 4)

    pairs = []
    for g in range(count):
        row = (g // 2 % 8) * 4 + g % 2 * 2 + g // 16
        free = list(range(count))
        for t in sorted(range(count), key=lambda t: -apart(g, row, g, t)):
            source = min(free, key=lambda source: apart(source, row, g, t))
            free.remove(source)
            pairs.append((source * count + row, g * count + t))
    return pairs


def front(acts, gate_weight, up_weight, routing):
    roll, steps, width = acts.shape
    half = gate_weight.shape[1] // 2
    core, side = lax.axis_index("c"), lax.axis_index("xl")
    swap = [(0, 1), (1, 0)]

    with jax.named_scope("share_weights"):
        gate_t, up_t = gate_weight.T, up_weight.T

        both = jnp.stack([gate_t, up_t])

        def columns(first, count):
            return lax.dynamic_slice_in_dim(both, first, count, 1)

        mine = columns(side * (half - MORE), half + MORE)
        got = lax.ppermute(columns((1 - side) * half, half), "xl", swap)
    with jax.named_scope("share_acts"):
        keep, give = pack(routing, core.reshape(1), acts)
        keep, give, got = lax.optimization_barrier((keep, give, got))
        keep = keep.reshape(roll * steps, -1)
        give = give.reshape(roll * steps, -1)
    with jax.named_scope("share_weights"):
        near = lax.all_gather(mine, "y", axis=0)
    with jax.named_scope("share_acts"):
        cross_same = lax.ppermute(keep, "xl", swap)
        cross_other = lax.ppermute(give, ("xl", "c", "xh"), around_x(lax.axis_size("xh")))
        sister = lax.ppermute(give, "c", swap)
    with jax.named_scope("share_weights"):
        far = lax.all_gather(got, "y", axis=0)
    with jax.named_scope("actor"):
        at_side = side.reshape(1)
        given = project(at_side, [sister, cross_other], near, far, FIRST)
        given = lax.ppermute(given, "c", swap)
        kept = project(at_side, [keep, cross_same], near, far, SECOND)
        return activate(at_side, kept, given, roll, half)


def body(acts, gate_weight, up_weight, section_weight, readout, lengths, routing):
    roll, steps, _ = acts.shape
    half = gate_weight.shape[1] // 2
    order = routing[0]
    hidden = front(acts, gate_weight, up_weight, routing)
    with jax.named_scope("route"):
        got = lax.all_to_all(hidden, G, split_axis=0, concat_axis=0, tiled=True)
        got = got.reshape(2, roll * steps, half)
    with jax.named_scope("section"):
        partial_value = jnp.dot(
            got[0], section_weight[0, :half], preferred_element_type=jnp.float32
        ) + jnp.dot(got[1], section_weight[0, half:], preferred_element_type=jnp.float32)
        partial_value = partial_value.astype(jnp.bfloat16).reshape(roll, steps, -1)
        pieces = lax.all_to_all(partial_value, T, split_axis=0, concat_axis=0, tiled=True)
        proj = jnp.sum(pieces.astype(jnp.float32), axis=0)
        score = jnp.sum(jax.nn.silu(proj) * readout[0][None, :], axis=1)
    with jax.named_scope("back"):
        score = jnp.broadcast_to(score[None, None, :], (roll, 1, steps))
        score = lax.all_to_all(score, G, split_axis=0, concat_axis=0, tiled=True)
        returned = lax.ppermute(score, G + T, across(roll)).reshape(roll, steps)
        here = order[:, None, None] == jnp.arange(roll)[None, None, :]
        placed = jnp.sum(jnp.where(here, returned[:, :, None], 0.0), axis=0)
        live = jnp.arange(steps)[:, None] < lengths[None, :]
        return jnp.where(live, placed, jnp.float32(0.0)).T


def solution(mesh):
    fine = Mesh(mesh.devices.reshape(2, 8, 2, 8, 4), G + T)
    in_specs = (
        P(G, None, None),
        P(G, T),
        P(G, T),
        P(G, T, None),
        P(G, None),
        P(G),
        P(G, None),
    )
    return jax.shard_map(
        body, mesh=fine, in_specs=in_specs, out_specs=P(G, None), check_vma=False
    )
```

```python
import jax
import jax.numpy as jnp
from jax import lax
from jax.experimental import pallas as pl
from jax.experimental.pallas import tpu as pltpu
from jax.sharding import Mesh, PartitionSpec as P

G = ("xl", "y", "c")
T = ("z", "xh")
LANES = 128
MORE = 32
FIRST = 50
SECOND = 16


def pack(routing, core, acts):
    roll, steps, width = acts.shape
    blocks = width // (2 * LANES)

    def kernel(routing_ref, core_ref, acts_ref, keep_ref, give_ref, rows, sem):
        copies = [
            pltpu.make_async_copy(acts_ref.at[routing_ref[0, at]], rows.at[at], sem.at[at])
            for at in range(roll)
        ]
        for copy in copies:
            copy.start()
        mine = core_ref[0] * LANES
        for at in range(roll):
            copies[at].wait()
            for block in range(blocks):
                to = pl.ds(block * LANES, LANES)
                keep_at = pl.multiple_of(2 * block * LANES + mine, LANES)
                give_at = pl.multiple_of(2 * block * LANES + LANES - mine, LANES)
                keep_ref[at, :, to] = rows[at, :, pl.ds(keep_at, LANES)]
                give_ref[at, :, to] = rows[at, :, pl.ds(give_at, LANES)]

    smem, vmem = pl.BlockSpec(memory_space=pltpu.SMEM), pl.BlockSpec(memory_space=pltpu.VMEM)
    out = jax.ShapeDtypeStruct((roll, steps, width // 2), acts.dtype)
    return pl.pallas_call(
        kernel,
        in_specs=[smem, smem, pl.BlockSpec(memory_space=pl.ANY)],
        out_specs=[vmem, vmem],
        out_shape=[out, out],
        scratch_shapes=[pltpu.VMEM(acts.shape, acts.dtype), pltpu.SemaphoreType.DMA((roll,))],
    )(routing, core, acts)


def project(side, rows_in, near, far, limit):
    rows, width = rows_in[0].shape
    sites, _, half, _ = far.shape
    n = len(rows_in)
    span = width // 2
    wide = -(-half // LANES) * LANES

    def kernel(side_ref, *refs):
        ins, weights, out = refs[:n], refs[n : n + 2], refs[n + 2]
        rows_at, weights_at, held, row_sem, weight_sem = refs[n + 3 :]
        near_first = pl.multiple_of(side_ref[0] * MORE, MORE)
        row_copies = [
            pltpu.make_async_copy(
                ins[at], rows_at.at[pl.ds(at * rows, rows)], row_sem.at[at]
            )
            for at in range(n)
        ]
        weight_copies = [
            pltpu.make_async_copy(
                weights[at].at[:, :, pl.ds(near_first if at == 0 else 0, half), :],
                weights_at.at[at],
                weight_sem.at[at],
            )
            for at in range(2)
        ]
        for copy in weight_copies + row_copies:
            copy.start()
        for at in (1, 0):
            weight_copies[at].wait()
            for part in range(2):
                for site in range(sites):
                    to = pl.ds(site * LANES, LANES)
                    held[at, part, :, to] = weights_at[at, site, part]
        for copy in row_copies:
            copy.wait()

        def product(at, part):
            first = side_ref[0] if at == 0 else 1 - side_ref[0]
            return lax.dot_general(
                rows_at[:, pl.ds(pl.multiple_of(first * span, span), span)],
                held[at, part],
                (((1,), (1,)), ((), ())),
                preferred_element_type=jnp.float32,
            )

        for part in range(2):
            value = product(0, part) + product(1, part)
            out[part, :, :, :half] = value.reshape(n, rows, half)
            out[part, :, :, half:] = jnp.zeros((n, rows, wide - half), jnp.float32)

    in_place = pl.BlockSpec(memory_space=pl.ANY)
    return pl.pallas_call(
        kernel,
        in_specs=[pl.BlockSpec(memory_space=pltpu.SMEM)] + [in_place] * (n + 2),
        out_specs=pl.BlockSpec(memory_space=pltpu.VMEM),
        out_shape=jax.ShapeDtypeStruct((2, n, rows, wide), jnp.float32),
        scratch_shapes=[
            pltpu.VMEM((n * rows, width), far.dtype),
            pltpu.VMEM((2, sites, 2, half, LANES), far.dtype),
            pltpu.VMEM((2, 2, half, span), far.dtype),
            pltpu.SemaphoreType.DMA((n,)),
            pltpu.SemaphoreType.DMA((2,)),
        ],
        compiler_params=pltpu.CompilerParams(vmem_limit_bytes=limit * 2**20),
        cost_estimate=pl.CostEstimate(
            flops=4 * n * rows * width * half, bytes_accessed=5 * 2**20, transcendentals=0
        ),
    )(side, *rows_in, near, far)


def activate(side, kept, given, roll, half):
    _, n, rows, wide = kept.shape
    steps = rows // roll

    def kernel(side_ref, kept_ref, given_ref, out_ref):
        gate = kept_ref[0, 0] + given_ref[0, 0]
        up = kept_ref[1, 0] + given_ref[1, 0]
        hidden = (gate * jax.nn.sigmoid(gate) * up)[:, :half]
        out_ref[:, 0] = hidden.reshape(roll, steps, half).astype(out_ref.dtype)

    spec = pl.BlockSpec((2, 1, rows, wide), lambda k, s: (0, k, 0, 0))
    return pl.pallas_call(
        kernel,
        grid_spec=pltpu.PrefetchScalarGridSpec(
            num_scalar_prefetch=1,
            grid=(n,),
            in_specs=[spec, spec],
            out_specs=pl.BlockSpec(
                (roll, 1, steps, half), lambda k, s: (0, k + s[0] - 2 * k * s[0], 0, 0)
            ),
        ),
        out_shape=jax.ShapeDtypeStruct((roll, n, steps, half), jnp.bfloat16),
        compiler_params=pltpu.CompilerParams(vmem_limit_bytes=16 * 2**20),
    )(side, kept, given)


def around_x(far):
    pairs = []
    for h in range(far):
        for c in range(2):
            pairs.append(((0 * 2 + c) * far + h, (1 * 2 + 1 - c) * far + (h - 1) % far))
            pairs.append(((1 * 2 + c) * far + h, (0 * 2 + 1 - c) * far + (h + 1) % far))
    return pairs


def across(count):
    def hops(a, b):
        return min((a - b) % 8, (b - a) % 8)

    def apart(source, row, g, t):
        along_x = hops(2 * (row % 4) + source // 16, 2 * (t % 4) + g // 16)
        return along_x + hops(source // 2 % 8, g // 2 % 8) + hops(row // 4, t // 4)

    pairs = []
    for g in range(count):
        row = (g // 2 % 8) * 4 + g % 2 * 2 + g // 16
        free = list(range(count))
        for t in sorted(range(count), key=lambda t: -apart(g, row, g, t)):
            source = min(free, key=lambda source: apart(source, row, g, t))
            free.remove(source)
            pairs.append((source * count + row, g * count + t))
    return pairs


def front(acts, gate_weight, up_weight, routing):
    roll, steps, width = acts.shape
    half = gate_weight.shape[1] // 2
    core, side = lax.axis_index("c"), lax.axis_index("xl")
    swap = [(0, 1), (1, 0)]

    with jax.named_scope("share_weights"):
        gate_t, up_t = gate_weight.T, up_weight.T

        both = jnp.stack([gate_t, up_t])

        def columns(first, count):
            return lax.dynamic_slice_in_dim(both, first, count, 1)

        mine = columns(side * (half - MORE), half + MORE)
        got = lax.ppermute(columns((1 - side) * half, half), "xl", swap)
    with jax.named_scope("share_acts"):
        keep, give = pack(routing, core.reshape(1), acts)
        keep, give, got = lax.optimization_barrier((keep, give, got))
        keep = keep.reshape(roll * steps, -1)
        give = give.reshape(roll * steps, -1)
    with jax.named_scope("share_weights"):
        near = lax.all_gather(mine, "y", axis=0)
    with jax.named_scope("share_acts"):
        cross_same = lax.ppermute(keep, "xl", swap)
        cross_other = lax.ppermute(give, ("xl", "c", "xh"), around_x(lax.axis_size("xh")))
        sister = lax.ppermute(give, "c", swap)
    with jax.named_scope("share_weights"):
        far = lax.all_gather(got, "y", axis=0)
    with jax.named_scope("actor"):
        at_side = side.reshape(1)
        given = project(at_side, [sister, cross_other], near, far, FIRST)
        given = lax.ppermute(given, "c", swap)
        kept = project(at_side, [keep, cross_same], near, far, SECOND)
        return activate(at_side, kept, given, roll, half)


def body(acts, gate_weight, up_weight, section_weight, readout, lengths, routing):
    roll, steps, _ = acts.shape
    half = gate_weight.shape[1] // 2
    order = routing[0]
    hidden = front(acts, gate_weight, up_weight, routing)
    with jax.named_scope("route"):
        got = lax.all_to_all(hidden, G, split_axis=0, concat_axis=0, tiled=True)
        got = got.reshape(2, roll * steps, half)
    with jax.named_scope("section"):
        partial_value = jnp.dot(
            got[0], section_weight[0, :half], preferred_element_type=jnp.float32
        ) + jnp.dot(got[1], section_weight[0, half:], preferred_element_type=jnp.float32)
        partial_value = partial_value.reshape(roll, steps, -1)
        pieces = lax.all_to_all(partial_value, T, split_axis=0, concat_axis=0, tiled=True)
        proj = jnp.sum(pieces, axis=0)
        score = jnp.sum(jax.nn.silu(proj) * readout[0][None, :], axis=1)
    with jax.named_scope("back"):
        score = jnp.broadcast_to(score[None, None, :], (roll, 1, steps))
        score = lax.all_to_all(score, G, split_axis=0, concat_axis=0, tiled=True)
        returned = lax.ppermute(score, G + T, across(roll)).reshape(roll, steps)
        here = order[:, None, None] == jnp.arange(roll)[None, None, :]
        placed = jnp.sum(jnp.where(here, returned[:, :, None], 0.0), axis=0)
        live = jnp.arange(steps)[:, None] < lengths[None, :]
        return jnp.where(live, placed, jnp.float32(0.0)).T


def solution(mesh):
    fine = Mesh(mesh.devices.reshape(2, 8, 2, 8, 4), G + T)
    in_specs = (
        P(G, None, None),
        P(G, T),
        P(G, T),
        P(G, T, None),
        P(G, None),
        P(G),
        P(G, None),
    )
    return jax.shard_map(
        body, mesh=fine, in_specs=in_specs, out_specs=P(G, None), check_vma=False
    )
```
